32 devices in a mesh: blk: 8 (over z, y), pen: 4 (over x, core).
Axes of the slice: x: 2, y: 2, z: 4, core: 2. Of those that a mesh axis runs over, the one named last changes fastest.
Arguments:
- snapshots: bfloat16 [4, 512, 512, 128], P(None, ('blk', 'pen')), may hold values from -110 to 110
- start_time: float32 [128, 64], replicated, may hold values from -6 to 6
- start_plane: float32 [512, 32], replicated, may hold values from -6 to 6
Outputs:
- time_basis: float32 [128, 64], replicated
- plane_basis: float32 [512, 32], replicated
- core_tensor: bfloat16 [4, 32, 32768], P(None, None, ('blk', 'pen'))
The draws below stay inside these ranges and needn't reach their ends.
All inputs are finite; a program needn't handle non-finite values.
Results may differ from the reference program's by a relative error of at most 0.005.
Values may be sent and summed in bfloat16 or wider, within the bound.
A program may use at most 64 MiB of HBM per device.

```python
import math
import jax
import jax.numpy as jnp
from jax import lax

VARS = 4
NX = 512
TSTEPS = 128
RANK_T = 64
RANK_X = 32
ITT = 3
ITX = 3
YZ = 512


def draw_snapshots(key, part):
    key_list = jax.random.split(key, 6)
    plane_index = jnp.arange(NX, dtype=jnp.float32).reshape(1, NX, 1, 1)
    cell_index = jnp.arange(YZ, dtype=jnp.float32).reshape(1, 1, YZ, 1)
    step_index = jnp.arange(TSTEPS, dtype=jnp.float32).reshape(1, 1, 1, TSTEPS)
    ramp_scale = jnp.exp(jnp.log(3.0) * (plane_index / max(NX - 1, 1) + cell_index / max(YZ - 1, 1)))
    rough_scale = jnp.exp(jax.random.uniform(key_list[0], (VARS, NX, YZ, 1), jnp.float32, 0.0, math.log(10.0)))
    noise_part = jnp.clip(jax.random.normal(key_list[1], (VARS, NX, YZ, TSTEPS), jnp.float32), -6.0, 6.0)
    step_scale = jnp.exp(jax.random.uniform(key_list[2], (VARS, 1, 1, TSTEPS), jnp.float32, 0.0, math.log(3.0)))
    wave_number = jax.random.randint(key_list[3], (VARS, 1, YZ, 1), 1, 9).astype(jnp.float32)
    angular_rate = jax.random.uniform(key_list[4], (VARS, 1, YZ, 1), jnp.float32, 0.05, 0.6)
    wave_phase = jax.random.uniform(key_list[5], (VARS, 1, YZ, 1), jnp.float32, -math.pi, math.pi)
    wave_part = jnp.cos(2.0 * math.pi * wave_number * plane_index / NX + angular_rate * step_index + wave_phase)
    result = rough_scale * ramp_scale * step_scale * (noise_part + 1.5 * wave_part) / 20.0
    return result.astype(jnp.bfloat16)


def gaussian(key, shape, width, bound, kind=jnp.bfloat16):
    return jnp.clip(width * jax.random.normal(key, shape, jnp.float32), -bound, bound).astype(kind)


def setup_inputs(seed: int = 0) -> dict:
    splits = jax.random.split(jax.random.key(seed), 4)
    return {
        "snapshots": draw_snapshots(jax.random.fold_in(splits[3], 71), 0),
        "start_time": gaussian(splits[1], (TSTEPS, RANK_T), 1.0, 6.0, jnp.float32),
        "start_plane": gaussian(splits[2], (NX, RANK_X), 1.0, 6.0, jnp.float32),
    }


HIGHEST = lax.Precision.HIGHEST

def orthonormal(matrix):
    for repeat in range(2):
        square_gram = jnp.dot(matrix.T, matrix, precision=HIGHEST)
        lower_factor = jnp.linalg.cholesky(square_gram)
        matrix = jax.scipy.linalg.solve_triangular(lower_factor, matrix.T, lower=True).T
    return matrix

def subspace(operator_gram, initial, sweeps):
    current = initial
    for repeat in range(sweeps):
        current = orthonormal(jnp.dot(operator_gram, current, precision=HIGHEST))
    return current

def reference(snapshots, start_time, start_plane):
    gram_time = jnp.zeros((TSTEPS, TSTEPS), jnp.float32)
    for variable in range(VARS):
        row_matrix = snapshots[variable].reshape(NX * YZ, TSTEPS)
        gram_time = gram_time + jnp.dot(row_matrix.T.astype(jnp.float32), row_matrix.astype(jnp.float32), preferred_element_type=jnp.float32)
    gram_time = gram_time / (VARS * NX * YZ)
    time_basis = subspace(gram_time, start_time, ITT)
    time_narrow = time_basis.astype(jnp.bfloat16)
    core_parts = []
    gram_plane = jnp.zeros((NX, NX), jnp.float32)
    for variable in range(VARS):
        row_matrix = snapshots[variable].reshape(NX * YZ, TSTEPS)
        core_part = jnp.dot(row_matrix.astype(jnp.float32), time_narrow.astype(jnp.float32), preferred_element_type=jnp.float32).astype(jnp.bfloat16)
        core_part = core_part.reshape(NX, YZ * RANK_T)
        gram_plane = gram_plane + jnp.dot(core_part.astype(jnp.float32), core_part.T.astype(jnp.float32), preferred_element_type=jnp.float32)
        core_parts.append(core_part)
    gram_plane = gram_plane / (VARS * YZ * RANK_T)
    plane_basis = subspace(gram_plane, start_plane, ITX)
    plane_narrow = plane_basis.astype(jnp.bfloat16)
    core_tensor = jnp.stack([jnp.dot(plane_narrow.T.astype(jnp.float32), core_part.astype(jnp.float32), preferred_element_type=jnp.float32).astype(jnp.bfloat16) for core_part in core_parts])
    return (time_basis, plane_basis, core_tensor)
```

```python
import functools

import jax
import jax.numpy as jnp
from jax import lax
from jax.experimental import pallas as pl
from jax.experimental.pallas import tpu as pltpu
from jax.sharding import PartitionSpec as P

ITT = 3
ITX = 3
LANES = 128
BLOCK = 8

HIGHEST = lax.Precision.HIGHEST
MESH = pl.DeviceIdType.MESH


def product(left, right, contract):
    return lax.dot_general(
        left, right, ((contract[:1], contract[1:]), ((), ())),
        precision=HIGHEST, preferred_element_type=jnp.float32,
    )


def inverse_factor(square):
    size = square.shape[0]
    rows = lax.broadcasted_iota(jnp.int32, (size, size), 0)
    columns = lax.broadcasted_iota(jnp.int32, (size, size), 1)
    wide = jnp.concatenate([square, (rows == columns).astype(jnp.float32)], axis=1)
    shape = (BLOCK, 2 * size)
    sublane = lax.broadcasted_iota(jnp.int32, shape, 0)
    done = []
    for first in range(0, size, BLOCK):
        panel = wide[first : first + BLOCK]
        entry = {
            (i, j): jnp.broadcast_to(panel[i : i + 1, first + j : first + j + 1], shape)
            for i in range(BLOCK)
            for j in range(i + 1)
        }
        scale, inverse = [], {}
        for j in range(BLOCK):
            scale.append(lax.rsqrt(entry[j, j]))
            for i in range(j + 1, BLOCK):
                entry[i, j] = entry[i, j] * scale[j]
            for i in range(j + 1, BLOCK):
                for t in range(j + 1, i + 1):
                    entry[i, t] = entry[i, t] - entry[i, j] * entry[t, j]
        for j in range(BLOCK):
            inverse[j, j] = scale[j]
            for i in range(j + 1, BLOCK):
                total = entry[i, j] * inverse[j, j]
                for t in range(j + 1, i):
                    total = total + entry[i, t] * inverse[t, j]
                inverse[i, j] = -scale[i] * total
        solved = jnp.zeros(shape, jnp.float32)
        for j in range(BLOCK):
            column = jnp.zeros(shape, jnp.float32)
            for i in range(j, BLOCK):
                column = jnp.where(sublane == i, inverse[i, j], column)
            solved = solved + column * jnp.broadcast_to(panel[j : j + 1], shape)
        done.append(solved)
        if first + BLOCK < size:
            wide = wide - product(solved, solved, (0, 0))[:size]
    return jnp.concatenate(done, axis=0)[:, size:]


def cholesky_round(rows):
    return product(inverse_factor(product(rows, rows, (1, 1))), rows, (1, 0))


def place(index):
    pens = lax.axis_size("pen")
    return (index // pens, lax.rem(index, pens))


def position():
    return lax.axis_index("blk") * lax.axis_size("pen") + lax.axis_index("pen")


def greet(count):
    me = position()
    barrier = pltpu.get_barrier_semaphore()

    def signal(step, carry):
        pl.semaphore_signal(
            barrier, inc=1, device_id=place(lax.rem(me + step, count)), device_id_type=MESH
        )
        return carry

    lax.fori_loop(1, count, signal, 0)
    pl.semaphore_wait(barrier, count - 1)


def sum_over_devices(count, parts, landed, gathered, sems):
    me = position()
    send_a, recv_a, send_b, recv_b = sems

    def scatter(step):
        there = lax.rem(me + step, count)
        return pltpu.make_async_remote_copy(
            src_ref=parts.at[there], dst_ref=landed.at[step],
            send_sem=send_a.at[step], recv_sem=recv_a.at[step],
            device_id=place(there), device_id_type=MESH,
        )

    def spread(step):
        there = lax.rem(me + step, count)
        return pltpu.make_async_remote_copy(
            src_ref=gathered.at[me], dst_ref=gathered.at[me],
            send_sem=send_b.at[step], recv_sem=recv_b.at[step],
            device_id=place(there), device_id_type=MESH,
        )

    def each(action):
        def body(step, carry):
            action(step)
            return carry

        lax.fori_loop(1, count, body, 0)

    each(lambda step: scatter(step).start())
    each(lambda step: scatter(step).wait())
    total = parts[me]
    for step in range(1, count):
        total = total + landed[step]
    gathered[me] = total
    each(lambda step: spread(step).start())
    each(lambda step: spread(step).wait())


def time_kernel(count, scale, parts, start, basis, landed, gathered, gram, *sems):
    greet(count)
    sum_over_devices(count, parts, landed, gathered, sems)
    depth = parts.shape[1]
    for piece in range(count):
        gram[piece * depth : (piece + 1) * depth, :] = gathered[piece] * scale
    basis[...] = start[...]

    def sweep(step, carry):
        basis[...] = cholesky_round(product(basis[...], gram[...], (1, 0)))
        return carry

    lax.fori_loop(0, ITT, sweep, 0)
    basis[...] = cholesky_round(basis[...])


def plane_kernel(count, scale, gram, start, basis, parts, landed, gathered, *sems):
    greet(count)
    rank, width = start.shape
    depth = parts.shape[2]
    basis[...] = start[...]

    def sweep(step, carry):
        share = product(basis[...], gram[...], (1, 0)) * scale
        stack = jnp.concatenate(
            [share[:, first : first + LANES] for first in range(0, width, LANES)], axis=0
        )
        for piece in range(count):
            parts[step, piece] = stack[piece * depth : (piece + 1) * depth]
        sum_over_devices(
            count, parts.at[step], landed.at[step], gathered.at[step],
            [sem.at[step] for sem in sems],
        )
        flat = jnp.concatenate([gathered[step, piece] for piece in range(count)], axis=0)
        total = jnp.concatenate(
            [flat[first : first + rank] for first in range(0, flat.shape[0], rank)], axis=1
        )
        basis[...] = cholesky_round(total)
        return carry

    lax.fori_loop(0, ITX, sweep, 0)
    basis[...] = cholesky_round(basis[...])


def in_vmem(number):
    return [pl.BlockSpec(memory_space=pltpu.VMEM)] * number


def time_subspace(share, start, scale, count):
    window = share.shape[0]
    depth = window // count
    slots = pltpu.VMEM((count, depth, window), jnp.float32)
    return pl.pallas_call(
        functools.partial(time_kernel, count, scale),
        out_shape=jax.ShapeDtypeStruct(start.shape, jnp.float32),
        in_specs=in_vmem(2),
        out_specs=pl.BlockSpec(memory_space=pltpu.VMEM),
        scratch_shapes=[slots, slots, pltpu.VMEM((window, window), jnp.float32)]
        + [pltpu.SemaphoreType.DMA((count,))] * 4,
        compiler_params=pltpu.CompilerParams(
            collective_id=0, has_side_effects=True, vmem_limit_bytes=32 << 20
        ),
    )(share.reshape(count, depth, window), start)


def plane_subspace(share, start, scale, count):
    rank, width = start.shape
    depth = rank * width // LANES // count
    slots = pltpu.VMEM((ITX, count, depth, LANES), jnp.float32)
    return pl.pallas_call(
        functools.partial(plane_kernel, count, scale),
        out_shape=jax.ShapeDtypeStruct(start.shape, jnp.float32),
        in_specs=in_vmem(2),
        out_specs=pl.BlockSpec(memory_space=pltpu.VMEM),
        scratch_shapes=[slots] * 3 + [pltpu.SemaphoreType.DMA((ITX, count))] * 4,
        compiler_params=pltpu.CompilerParams(
            collective_id=1, has_side_effects=True, vmem_limit_bytes=32 << 20
        ),
    )(share, start)


def on_device(snapshots, start_time, start_plane):
    variables, planes, cell_count, window = snapshots.shape
    devices_all = lax.axis_size("blk") * lax.axis_size("pen")
    row_matrix = snapshots.reshape(variables * planes * cell_count, window)
    partial_time = jnp.dot(row_matrix.T, row_matrix, preferred_element_type=jnp.float32)
    time_rows = time_subspace(
        partial_time,
        start_time.T,
        1.0 / float(variables * planes * cell_count * devices_all),
        devices_all,
    )
    time_basis = time_rows.T
    time_narrow = time_basis.astype(jnp.bfloat16)
    zero_block = jnp.zeros_like(time_narrow)
    pair_basis = jnp.stack(
        [
            jnp.concatenate([time_narrow, zero_block], axis=1),
            jnp.concatenate([zero_block, time_narrow], axis=1),
        ]
    )
    pair_count = cell_count // 2
    paired = snapshots.reshape(variables, planes, pair_count, 2, window)
    core_time = jnp.einsum(
        "vxpqt,qtl->vxpl", paired, pair_basis, preferred_element_type=jnp.float32
    ).astype(jnp.bfloat16)
    pencils = lax.all_to_all(core_time, ("blk", "pen"), split_axis=2, concat_axis=1, tiled=True)
    column_total = float(variables * pencils.shape[2] * pencils.shape[3] * devices_all)
    partial_plane = jnp.einsum(
        "vxpl,vypl->xy", pencils, pencils, preferred_element_type=jnp.float32
    )
    plane_rows = plane_subspace(partial_plane, start_plane.T, 1.0 / column_total, devices_all)
    plane_basis = plane_rows.T
    plane_narrow = plane_basis.astype(jnp.bfloat16)
    core_blocks = jnp.einsum(
        "xk,vxpl->vkpl", plane_narrow, pencils, preferred_element_type=jnp.float32
    ).astype(jnp.bfloat16)
    core_tensor = core_blocks.reshape(variables, core_blocks.shape[1], -1)
    return (time_basis, plane_basis, core_tensor)


def solution(mesh):
    return jax.shard_map(
        on_device,
        mesh=mesh,
        in_specs=(P(None, ("blk", "pen"), None, None), P(), P()),
        out_specs=(P(), P(), P(None, None, ("blk", "pen"))),
        check_vma=False,
    )
```

```python
import functools

import jax
import jax.numpy as jnp
from jax import lax
from jax.experimental import pallas as pl
from jax.experimental.pallas import tpu as pltpu
from jax.sharding import PartitionSpec as P

ITT = 3
ITX = 3
LANES = 128
BLOCK = 8

HIGHEST = lax.Precision.HIGHEST
MESH = pl.DeviceIdType.MESH


def product(left, right, contract):
    return lax.dot_general(
        left, right, ((contract[:1], contract[1:]), ((), ())),
        precision=HIGHEST, preferred_element_type=jnp.float32,
    )


def inverse_factor(square):
    size = square.shape[0]
    rows = lax.broadcasted_iota(jnp.int32, (size, size), 0)
    columns = lax.broadcasted_iota(jnp.int32, (size, size), 1)
    wide = jnp.concatenate([square, (rows == columns).astype(jnp.float32)], axis=1)
    shape = (BLOCK, 2 * size)
    sublane = lax.broadcasted_iota(jnp.int32, shape, 0)
    panels = [wide[first : first + BLOCK] for first in range(0, size, BLOCK)]
    done = []
    for number, panel in enumerate(panels):
        first = number * BLOCK
        spread = {
            (later, j): jnp.broadcast_to(panels[later][:, first + j : first + j + 1], shape)
            for later in range(number, len(panels))
            for j in range(BLOCK)
        }
        row = [jnp.broadcast_to(panel[j : j + 1], shape) for j in range(BLOCK)]
        entry = {
            (i, j): jnp.broadcast_to(spread[number, j][i : i + 1], shape)
            for i in range(BLOCK)
            for j in range(i + 1)
        }
        scale, inverse = [], {}
        for j in range(BLOCK):
            scale.append(lax.rsqrt(entry[j, j]))
            for i in range(j + 1, BLOCK):
                entry[i, j] = entry[i, j] * scale[j]
            for i in range(j + 1, BLOCK):
                for t in range(j + 1, i + 1):
                    entry[i, t] = entry[i, t] - entry[i, j] * entry[t, j]
        for j in range(BLOCK):
            inverse[j, j] = scale[j]
            for i in range(j + 1, BLOCK):
                total = entry[i, j] * inverse[j, j]
                for t in range(j + 1, i):
                    total = total + entry[i, t] * inverse[t, j]
                inverse[i, j] = -scale[i] * total
        solved = [
            sum(inverse[i, t] * row[t] for t in range(i + 1)) for i in range(BLOCK)
        ]
        if number + 1 < len(panels):
            twice = [
                sum(inverse[i, t] * solved[i] for i in range(t, BLOCK)) for t in range(BLOCK)
            ]
            for later in range(number + 1, len(panels)):
                panels[later] = panels[later] - sum(
                    spread[later, t] * twice[t] for t in range(BLOCK)
                )
        joined = solved[0]
        for i in range(1, BLOCK):
            joined = jnp.where(sublane == i, solved[i], joined)
        done.append(joined)
    return jnp.concatenate(done, axis=0)[:, size:]


def cholesky_round(rows):
    return product(inverse_factor(product(rows, rows, (1, 1))), rows, (1, 0))


def place(index):
    pens = lax.axis_size("pen")
    return (index // pens, lax.rem(index, pens))


def position():
    return lax.axis_index("blk") * lax.axis_size("pen") + lax.axis_index("pen")


def greet(count):
    me = position()
    barrier = pltpu.get_barrier_semaphore()

    def signal(step, carry):
        pl.semaphore_signal(
            barrier, inc=1, device_id=place(lax.rem(me + step, count)), device_id_type=MESH
        )
        return carry

    lax.fori_loop(1, count, signal, 0)
    pl.semaphore_wait(barrier, count - 1)


def sum_over_devices(count, parts, landed, gathered, sems):
    me = position()
    send_a, recv_a, send_b, recv_b = sems

    def scatter(step):
        there = lax.rem(me + step, count)
        return pltpu.make_async_remote_copy(
            src_ref=parts.at[there], dst_ref=landed.at[step],
            send_sem=send_a.at[step], recv_sem=recv_a.at[step],
            device_id=place(there), device_id_type=MESH,
        )

    def spread(step):
        there = lax.rem(me + step, count)
        return pltpu.make_async_remote_copy(
            src_ref=gathered.at[me], dst_ref=gathered.at[me],
            send_sem=send_b.at[step], recv_sem=recv_b.at[step],
            device_id=place(there), device_id_type=MESH,
        )

    def each(action):
        def body(step, carry):
            action(step)
            return carry

        lax.fori_loop(1, count, body, 0)

    each(lambda step: scatter(step).start())
    each(lambda step: scatter(step).wait())
    total = parts[me]
    for step in range(1, count):
        total = total + landed[step]
    gathered[me] = total
    each(lambda step: spread(step).start())
    each(lambda step: spread(step).wait())


def time_kernel(count, scale, share, start, basis, parts, landed, gathered, gram, *sems):
    depth = parts.shape[1]
    for piece in range(count):
        parts[piece] = share[piece * depth : (piece + 1) * depth, :]
    greet(count)
    sum_over_devices(count, parts, landed, gathered, sems)
    for piece in range(count):
        gram[piece * depth : (piece + 1) * depth, :] = gathered[piece] * scale
    basis[...] = start[...]

    def sweep(step, carry):
        basis[...] = cholesky_round(product(basis[...], gram[...], (1, 0)))
        return carry

    lax.fori_loop(0, ITT, sweep, 0)
    basis[...] = cholesky_round(basis[...])


def plane_kernel(count, scale, gram, start, basis, parts, landed, gathered, *sems):
    greet(count)
    rank, width = start.shape
    depth = parts.shape[2]
    basis[...] = start[...]

    def sweep(step, carry):
        share = product(basis[...], gram[...], (1, 0)) * scale
        stack = jnp.concatenate(
            [share[:, first : first + LANES] for first in range(0, width, LANES)], axis=0
        )
        for piece in range(count):
            parts[step, piece] = stack[piece * depth : (piece + 1) * depth]
        sum_over_devices(
            count, parts.at[step], landed.at[step], gathered.at[step],
            [sem.at[step] for sem in sems],
        )
        flat = jnp.concatenate([gathered[step, piece] for piece in range(count)], axis=0)
        total = jnp.concatenate(
            [flat[first : first + rank] for first in range(0, flat.shape[0], rank)], axis=1
        )
        basis[...] = cholesky_round(total)
        return carry

    lax.fori_loop(0, ITX, sweep, 0)
    basis[...] = cholesky_round(basis[...])


def in_vmem(number):
    return [pl.BlockSpec(memory_space=pltpu.VMEM)] * number


def time_subspace(share, start, scale, count):
    window = share.shape[0]
    depth = window // count
    slots = pltpu.VMEM((count, depth, window), jnp.float32)
    return pl.pallas_call(
        functools.partial(time_kernel, count, scale),
        out_shape=jax.ShapeDtypeStruct(start.shape, jnp.float32),
        in_specs=in_vmem(2),
        out_specs=pl.BlockSpec(memory_space=pltpu.VMEM),
        scratch_shapes=[slots, slots, slots, pltpu.VMEM((window, window), jnp.float32)]
        + [pltpu.SemaphoreType.DMA((count,))] * 4,
        compiler_params=pltpu.CompilerParams(
            collective_id=0, has_side_effects=True, vmem_limit_bytes=32 << 20
        ),
        cost_estimate=pl.CostEstimate(
            flops=60_000_000_000, bytes_accessed=100_000_000, transcendentals=0
        ),
    )(share, start)


def plane_subspace(share, start, scale, count):
    rank, width = start.shape
    depth = rank * width // LANES // count
    slots = pltpu.VMEM((ITX, count, depth, LANES), jnp.float32)
    return pl.pallas_call(
        functools.partial(plane_kernel, count, scale),
        out_shape=jax.ShapeDtypeStruct(start.shape, jnp.float32),
        in_specs=in_vmem(2),
        out_specs=pl.BlockSpec(memory_space=pltpu.VMEM),
        scratch_shapes=[slots] * 3 + [pltpu.SemaphoreType.DMA((ITX, count))] * 4,
        compiler_params=pltpu.CompilerParams(
            collective_id=1, has_side_effects=True, vmem_limit_bytes=32 << 20
        ),
    )(share, start)


def on_device(snapshots, start_time, start_plane):
    variables, planes, cell_count, window = snapshots.shape
    devices_all = lax.axis_size("blk") * lax.axis_size("pen")
    axes = ("blk", "pen")
    early = variables // 4
    early_cells = lax.all_to_all(
        snapshots[:early], axes, split_axis=2, concat_axis=1, tiled=True
    )
    row_matrix = snapshots.reshape(variables * planes * cell_count, window)
    partial_time = jnp.dot(row_matrix.T, row_matrix, preferred_element_type=jnp.float32)
    time_rows = time_subspace(
        partial_time,
        start_time.T,
        1.0 / float(variables * planes * cell_count * devices_all),
        devices_all,
    )
    time_basis = time_rows.T
    time_narrow = time_basis.astype(jnp.bfloat16)
    zero_block = jnp.zeros_like(time_narrow)
    pair_basis = jnp.stack(
        [
            jnp.concatenate([time_narrow, zero_block], axis=1),
            jnp.concatenate([zero_block, time_narrow], axis=1),
        ]
    )

    def truncate(cells):
        paired = cells.reshape(cells.shape[0], cells.shape[1], -1, 2, window)
        return jnp.einsum(
            "vxpqt,qtl->vxpl", paired, pair_basis, preferred_element_type=jnp.float32
        ).astype(jnp.bfloat16)

    pencils = [
        lax.all_to_all(
            truncate(snapshots[variable : variable + 1]),
            axes, split_axis=2, concat_axis=1, tiled=True,
        )
        for variable in range(early, variables)
    ]
    if early:
        pencils.insert(0, truncate(early_cells))
    column_total = float(variables * pencils[0].shape[2] * pencils[0].shape[3] * devices_all)
    partial_plane = sum(
        jnp.einsum("vxpl,vypl->xy", pencil, pencil, preferred_element_type=jnp.float32)
        for pencil in pencils
    )
    plane_rows = plane_subspace(partial_plane, start_plane.T, 1.0 / column_total, devices_all)
    plane_basis = plane_rows.T
    plane_narrow = plane_basis.astype(jnp.bfloat16)
    core_blocks = jnp.concatenate(
        [
            jnp.einsum("xk,vxpl->vkpl", plane_narrow, pencil, preferred_element_type=jnp.float32)
            for pencil in pencils
        ]
    ).astype(jnp.bfloat16)
    core_tensor = core_blocks.reshape(variables, core_blocks.shape[1], -1)
    return (time_basis, plane_basis, core_tensor)


def solution(mesh):
    return jax.shard_map(
        on_device,
        mesh=mesh,
        in_specs=(P(None, ("blk", "pen"), None, None), P(), P()),
        out_specs=(P(), P(), P(None, None, ("blk", "pen"))),
        check_vma=False,
    )
```

```python
import functools

import jax
import jax.numpy as jnp
from jax import lax
from jax.experimental import pallas as pl
from jax.experimental.pallas import tpu as pltpu
from jax.sharding import PartitionSpec as P

ITT = 3
ITX = 3
LANES = 128
BLOCK = 8

HIGHEST = lax.Precision.HIGHEST
MESH = pl.DeviceIdType.MESH


def product(left, right, contract):
    return lax.dot_general(
        left, right, ((contract[:1], contract[1:]), ((), ())),
        precision=HIGHEST, preferred_element_type=jnp.float32,
    )


def inverse_factor(square):
    size = square.shape[0]
    rows = lax.broadcasted_iota(jnp.int32, (size, size), 0)
    columns = lax.broadcasted_iota(jnp.int32, (size, size), 1)
    wide = jnp.concatenate([square, (rows == columns).astype(jnp.float32)], axis=1)
    shape = (BLOCK, 2 * size)
    sublane = lax.broadcasted_iota(jnp.int32, shape, 0)
    panels = [wide[first : first + BLOCK] for first in range(0, size, BLOCK)]
    done = []
    for number, panel in enumerate(panels):
        first = number * BLOCK
        spread = {
            (later, j): jnp.broadcast_to(panels[later][:, first + j : first + j + 1], shape)
            for later in range(number, len(panels))
            for j in range(BLOCK)
        }
        row = [jnp.broadcast_to(panel[j : j + 1], shape) for j in range(BLOCK)]
        entry = {
            (i, j): jnp.broadcast_to(spread[number, j][i : i + 1], shape)
            for i in range(BLOCK)
            for j in range(i + 1)
        }
        scale, inverse = [], {}
        for j in range(BLOCK):
            scale.append(lax.rsqrt(entry[j, j]))
            for i in range(j + 1, BLOCK):
                entry[i, j] = entry[i, j] * scale[j]
            for i in range(j + 1, BLOCK):
                for t in range(j + 1, i + 1):
                    entry[i, t] = entry[i, t] - entry[i, j] * entry[t, j]
        for j in range(BLOCK):
            inverse[j, j] = scale[j]
            for i in range(j + 1, BLOCK):
                total = entry[i, j] * inverse[j, j]
                for t in range(j + 1, i):
                    total = total + entry[i, t] * inverse[t, j]
                inverse[i, j] = -scale[i] * total
        solved = [
            sum(inverse[i, t] * row[t] for t in range(i + 1)) for i in range(BLOCK)
        ]
        if number + 1 < len(panels):
            twice = [
                sum(inverse[i, t] * solved[i] for i in range(t, BLOCK)) for t in range(BLOCK)
            ]
            for later in range(number + 1, len(panels)):
                panels[later] = panels[later] - sum(
                    spread[later, t] * twice[t] for t in range(BLOCK)
                )
        joined = solved[0]
        for i in range(1, BLOCK):
            joined = jnp.where(sublane == i, solved[i], joined)
        done.append(joined)
    return jnp.concatenate(done, axis=0)[:, size:]


def cholesky_round(rows):
    return product(inverse_factor(product(rows, rows, (1, 1))), rows, (1, 0))


def place(index):
    pens = lax.axis_size("pen")
    return (index // pens, lax.rem(index, pens))


def position():
    return lax.axis_index("blk") * lax.axis_size("pen") + lax.axis_index("pen")


def greet(count):
    me = position()
    barrier = pltpu.get_barrier_semaphore()

    def signal(step, carry):
        pl.semaphore_signal(
            barrier, inc=1, device_id=place(lax.rem(me + step, count)), device_id_type=MESH
        )
        return carry

    lax.fori_loop(1, count, signal, 0)
    pl.semaphore_wait(barrier, count - 1)


def sum_over_devices(count, parts, landed, gathered, sems):
    me = position()
    send_a, recv_a, send_b, recv_b = sems

    def scatter(step):
        there = lax.rem(me + step, count)
        return pltpu.make_async_remote_copy(
            src_ref=parts.at[there], dst_ref=landed.at[step],
            send_sem=send_a.at[step], recv_sem=recv_a.at[step],
            device_id=place(there), device_id_type=MESH,
        )

    def spread(step):
        there = lax.rem(me + step, count)
        return pltpu.make_async_remote_copy(
            src_ref=gathered.at[me], dst_ref=gathered.at[me],
            send_sem=send_b.at[step], recv_sem=recv_b.at[step],
            device_id=place(there), device_id_type=MESH,
        )

    def each(action):
        def body(step, carry):
            action(step)
            return carry

        lax.fori_loop(1, count, body, 0)

    each(lambda step: scatter(step).start())
    each(lambda step: scatter(step).wait())
    total = parts[me]
    for step in range(1, count):
        total = total + landed[step]
    gathered[me] = total
    each(lambda step: spread(step).start())
    each(lambda step: spread(step).wait())


def time_kernel(count, scale, share, start, basis, parts, landed, gathered, gram, *sems):
    depth = parts.shape[1]
    for piece in range(count):
        parts[piece] = share[piece * depth : (piece + 1) * depth, :]
    greet(count)
    sum_over_devices(count, parts, landed, gathered, sems)
    for piece in range(count):
        gram[piece * depth : (piece + 1) * depth, :] = gathered[piece] * scale
    basis[...] = start[...]

    def sweep(step, carry):
        basis[...] = cholesky_round(product(basis[...], gram[...], (1, 0)))
        return carry

    lax.fori_loop(0, ITT, sweep, 0)
    basis[...] = cholesky_round(basis[...])


def plane_kernel(count, scale, gram, start, basis, parts, landed, gathered, *sems):
    greet(count)
    rank, width = start.shape
    depth = parts.shape[2]
    basis[...] = start[...]

    def sweep(step, carry):
        share = product(basis[...], gram[...], (1, 0)) * scale
        stack = jnp.concatenate(
            [share[:, first : first + LANES] for first in range(0, width, LANES)], axis=0
        )
        for piece in range(count):
            parts[step, piece] = stack[piece * depth : (piece + 1) * depth]
        sum_over_devices(
            count, parts.at[step], landed.at[step], gathered.at[step],
            [sem.at[step] for sem in sems],
        )
        flat = jnp.concatenate([gathered[step, piece] for piece in range(count)], axis=0)
        total = jnp.concatenate(
            [flat[first : first + rank] for first in range(0, flat.shape[0], rank)], axis=1
        )
        basis[...] = cholesky_round(total)
        return carry

    lax.fori_loop(0, ITX, sweep, 0)
    basis[...] = cholesky_round(basis[...])


def in_vmem(number):
    return [pl.BlockSpec(memory_space=pltpu.VMEM)] * number


def time_subspace(share, start, scale, count):
    window = share.shape[0]
    depth = window // count
    slots = pltpu.VMEM((count, depth, window), jnp.float32)
    return pl.pallas_call(
        functools.partial(time_kernel, count, scale),
        out_shape=jax.ShapeDtypeStruct(start.shape, jnp.float32),
        in_specs=in_vmem(2),
        out_specs=pl.BlockSpec(memory_space=pltpu.VMEM),
        scratch_shapes=[slots, slots, slots, pltpu.VMEM((window, window), jnp.float32)]
        + [pltpu.SemaphoreType.DMA((count,))] * 4,
        compiler_params=pltpu.CompilerParams(
            collective_id=0, has_side_effects=True, vmem_limit_bytes=32 << 20
        ),
    )(share, start)


def plane_subspace(share, start, scale, count):
    rank, width = start.shape
    depth = rank * width // LANES // count
    slots = pltpu.VMEM((ITX, count, depth, LANES), jnp.float32)
    return pl.pallas_call(
        functools.partial(plane_kernel, count, scale),
        out_shape=jax.ShapeDtypeStruct(start.shape, jnp.float32),
        in_specs=in_vmem(2),
        out_specs=pl.BlockSpec(memory_space=pltpu.VMEM),
        scratch_shapes=[slots] * 3 + [pltpu.SemaphoreType.DMA((ITX, count))] * 4,
        compiler_params=pltpu.CompilerParams(
            collective_id=1, has_side_effects=True, vmem_limit_bytes=32 << 20
        ),
    )(share, start)


def exchange_kernel(count, snapshots, wide, pencils, parts, send, recv):
    greet(count)
    me = position()
    variables, planes, cells, window = snapshots.shape
    own = cells // count
    half = own // 2
    blocks = variables * planes

    def truncated(owner):
        here = pl.ds(pl.multiple_of(owner * own, own), own)
        rows = snapshots[:, :, here, :].reshape(blocks * own, window)
        pair = jnp.dot(rows, wide[...], preferred_element_type=jnp.float32)
        pair = pair.reshape(blocks, own, pair.shape[1])
        lanes = pair.shape[2] // 2
        packed = pair[:, :half, :lanes] + pair[:, half:, lanes:]
        return packed.reshape(blocks * half, lanes).astype(jnp.bfloat16)

    def copy(step):
        there = lax.rem(me + step, count)
        return pltpu.make_async_remote_copy(
            src_ref=parts.at[there], dst_ref=pencils.at[me],
            send_sem=send.at[step], recv_sem=recv.at[step],
            device_id=place(there), device_id_type=MESH,
        )

    def begin(step, carry):
        there = lax.rem(me + step, count)
        parts[there] = truncated(there)
        copy(step).start()
        return carry

    def finish(step, carry):
        copy(step).wait()
        return carry

    lax.fori_loop(1, count, begin, 0)
    pencils[me] = truncated(me)
    lax.fori_loop(1, count, finish, 0)


def exchange(snapshots, narrow, count):
    variables, planes, cells, window = snapshots.shape
    zero = jnp.zeros_like(narrow)
    wide = jnp.concatenate([narrow, zero, zero, narrow], axis=1)
    half = cells // count // 2
    shape = (count, variables * planes * half, 2 * narrow.shape[1])
    pencils = pl.pallas_call(
        functools.partial(exchange_kernel, count),
        out_shape=jax.ShapeDtypeStruct(shape, jnp.bfloat16),
        in_specs=in_vmem(2),
        out_specs=pl.BlockSpec(memory_space=pltpu.VMEM),
        scratch_shapes=[pltpu.VMEM(shape, jnp.bfloat16)]
        + [pltpu.SemaphoreType.DMA((count,))] * 2,
        compiler_params=pltpu.CompilerParams(
            collective_id=2, has_side_effects=True, vmem_limit_bytes=40 << 20
        ),
    )(snapshots, wide)
    pencils = pencils.reshape(count, variables, planes, half, shape[2])
    return pencils.transpose(1, 0, 2, 3, 4).reshape(variables, count * planes, half, shape[2])


def on_device(snapshots, start_time, start_plane):
    variables, planes, cell_count, window = snapshots.shape
    devices_all = lax.axis_size("blk") * lax.axis_size("pen")
    row_matrix = snapshots.reshape(variables * planes * cell_count, window)
    partial_time = jnp.dot(row_matrix.T, row_matrix, preferred_element_type=jnp.float32)
    time_rows = time_subspace(
        partial_time,
        start_time.T,
        1.0 / float(variables * planes * cell_count * devices_all),
        devices_all,
    )
    time_basis = time_rows.T
    time_narrow = time_basis.astype(jnp.bfloat16)
    pencils = exchange(snapshots, time_narrow, devices_all)
    column_total = float(variables * pencils.shape[2] * pencils.shape[3] * devices_all)
    partial_plane = jnp.einsum(
        "vxpl,vypl->xy", pencils, pencils, preferred_element_type=jnp.float32
    )
    plane_rows = plane_subspace(partial_plane, start_plane.T, 1.0 / column_total, devices_all)
    plane_basis = plane_rows.T
    plane_narrow = plane_basis.astype(jnp.bfloat16)
    core_blocks = jnp.einsum(
        "xk,vxpl->vkpl", plane_narrow, pencils, preferred_element_type=jnp.float32
    ).astype(jnp.bfloat16)
    rank = plane_narrow.shape[1]
    core_blocks = core_blocks.reshape(variables, rank, pencils.shape[2], 2, -1)
    core_tensor = core_blocks.transpose(0, 1, 3, 2, 4).reshape(variables, rank, -1)
    return (time_basis, plane_basis, core_tensor)


def solution(mesh):
    return jax.shard_map(
        on_device,
        mesh=mesh,
        in_specs=(P(None, ("blk", "pen"), None, None), P(), P()),
        out_specs=(P(), P(), P(None, None, ("blk", "pen"))),
        check_vma=False,
    )
```

```python
import functools

import jax
import jax.numpy as jnp
from jax import lax
from jax.experimental import pallas as pl
from jax.experimental.pallas import tpu as pltpu
from jax.sharding import PartitionSpec as P

ITT = 3
ITX = 3
LANES = 128
BLOCK = 8

HIGHEST = lax.Precision.HIGHEST
MESH = pl.DeviceIdType.MESH


def product(left, right, contract):
    return lax.dot_general(
        left, right, ((contract[:1], contract[1:]), ((), ())),
        precision=HIGHEST, preferred_element_type=jnp.float32,
    )


def inverse_factor(square):
    size = square.shape[0]
    rows = lax.broadcasted_iota(jnp.int32, (size, size), 0)
    columns = lax.broadcasted_iota(jnp.int32, (size, size), 1)
    wide = jnp.concatenate([square, (rows == columns).astype(jnp.float32)], axis=1)
    shape = (BLOCK, 2 * size)
    sublane = lax.broadcasted_iota(jnp.int32, shape, 0)
    panels = [wide[first : first + BLOCK] for first in range(0, size, BLOCK)]
    done = []
    for number, panel in enumerate(panels):
        first = number * BLOCK
        spread = {
            (later, j): jnp.broadcast_to(panels[later][:, first + j : first + j + 1], shape)
            for later in range(number, len(panels))
            for j in range(BLOCK)
        }
        row = [jnp.broadcast_to(panel[j : j + 1], shape) for j in range(BLOCK)]
        entry = {
            (i, j): jnp.broadcast_to(spread[number, j][i : i + 1], shape)
            for i in range(BLOCK)
            for j in range(i + 1)
        }
        scale, inverse = [], {}
        for j in range(BLOCK):
            scale.append(lax.rsqrt(entry[j, j]))
            for i in range(j + 1, BLOCK):
                entry[i, j] = entry[i, j] * scale[j]
            for i in range(j + 1, BLOCK):
                for t in range(j + 1, i + 1):
                    entry[i, t] = entry[i, t] - entry[i, j] * entry[t, j]
        for j in range(BLOCK):
            inverse[j, j] = scale[j]
            for i in range(j + 1, BLOCK):
                total = entry[i, j] * inverse[j, j]
                for t in range(j + 1, i):
                    total = total + entry[i, t] * inverse[t, j]
                inverse[i, j] = -scale[i] * total
        solved = [
            sum(inverse[i, t] * row[t] for t in range(i + 1)) for i in range(BLOCK)
        ]
        if number + 1 < len(panels):
            twice = [
                sum(inverse[i, t] * solved[i] for i in range(t, BLOCK)) for t in range(BLOCK)
            ]
            for later in range(number + 1, len(panels)):
                panels[later] = panels[later] - sum(
                    spread[later, t] * twice[t] for t in range(BLOCK)
                )
        joined = solved[0]
        for i in range(1, BLOCK):
            joined = jnp.where(sublane == i, solved[i], joined)
        done.append(joined)
    return jnp.concatenate(done, axis=0)[:, size:]


def cholesky_round(rows):
    return product(inverse_factor(product(rows, rows, (1, 1))), rows, (1, 0))


def place(index):
    pens = lax.axis_size("pen")
    return (index // pens, lax.rem(index, pens))


def position():
    return lax.axis_index("blk") * lax.axis_size("pen") + lax.axis_index("pen")


def greet(count):
    me = position()
    barrier = pltpu.get_barrier_semaphore()

    def signal(step, carry):
        pl.semaphore_signal(
            barrier, inc=1, device_id=place(lax.rem(me + step, count)), device_id_type=MESH
        )
        return carry

    lax.fori_loop(1, count, signal, 0)
    pl.semaphore_wait(barrier, count - 1)


def sum_over_devices(count, parts, landed, gathered, sems):
    me = position()
    send_a, recv_a, send_b, recv_b = sems

    def scatter(step):
        there = lax.rem(me + step, count)
        return pltpu.make_async_remote_copy(
            src_ref=parts.at[there], dst_ref=landed.at[step],
            send_sem=send_a.at[step], recv_sem=recv_a.at[step],
            device_id=place(there), device_id_type=MESH,
        )

    def spread(step):
        there = lax.rem(me + step, count)
        return pltpu.make_async_remote_copy(
            src_ref=gathered.at[me], dst_ref=gathered.at[me],
            send_sem=send_b.at[step], recv_sem=recv_b.at[step],
            device_id=place(there), device_id_type=MESH,
        )

    def each(action):
        def body(step, carry):
            action(step)
            return carry

        lax.fori_loop(1, count, body, 0)

    each(lambda step: scatter(step).start())
    each(lambda step: scatter(step).wait())
    total = parts[me]
    for step in range(1, count):
        total = total + landed[step]
    gathered[me] = total
    each(lambda step: spread(step).start())
    each(lambda step: spread(step).wait())


def time_kernel(count, scale, share, start, basis, parts, landed, gathered, gram, *sems):
    depth = parts.shape[1]
    for piece in range(count):
        parts[piece] = share[piece * depth : (piece + 1) * depth, :]
    greet(count)
    sum_over_devices(count, parts, landed, gathered, sems)
    for piece in range(count):
        gram[piece * depth : (piece + 1) * depth, :] = gathered[piece] * scale
    basis[...] = start[...]

    def sweep(step, carry):
        basis[...] = cholesky_round(product(basis[...], gram[...], (1, 0)))
        return carry

    lax.fori_loop(0, ITT, sweep, 0)
    basis[...] = cholesky_round(basis[...])


def plane_kernel(count, scale, gram, start, basis, parts, landed, gathered, *sems):
    greet(count)
    rank, width = start.shape
    depth = parts.shape[2]
    basis[...] = start[...]

    def sweep(step, carry):
        share = product(basis[...], gram[...], (1, 0)) * scale
        stack = jnp.concatenate(
            [share[:, first : first + LANES] for first in range(0, width, LANES)], axis=0
        )
        for piece in range(count):
            parts[step, piece] = stack[piece * depth : (piece + 1) * depth]
        sum_over_devices(
            count, parts.at[step], landed.at[step], gathered.at[step],
            [sem.at[step] for sem in sems],
        )
        flat = jnp.concatenate([gathered[step, piece] for piece in range(count)], axis=0)
        total = jnp.concatenate(
            [flat[first : first + rank] for first in range(0, flat.shape[0], rank)], axis=1
        )
        basis[...] = cholesky_round(total)
        return carry

    lax.fori_loop(0, ITX, sweep, 0)
    basis[...] = cholesky_round(basis[...])


def in_vmem(number):
    return [pl.BlockSpec(memory_space=pltpu.VMEM)] * number


def time_subspace(share, start, scale, count):
    window = share.shape[0]
    depth = window // count
    slots = pltpu.VMEM((count, depth, window), jnp.float32)
    return pl.pallas_call(
        functools.partial(time_kernel, count, scale),
        out_shape=jax.ShapeDtypeStruct(start.shape, jnp.float32),
        in_specs=in_vmem(2),
        out_specs=pl.BlockSpec(memory_space=pltpu.VMEM),
        scratch_shapes=[slots, slots, slots, pltpu.VMEM((window, window), jnp.float32)]
        + [pltpu.SemaphoreType.DMA((count,))] * 4,
        compiler_params=pltpu.CompilerParams(
            collective_id=0, has_side_effects=True, vmem_limit_bytes=32 << 20
        ),
    )(share, start)


def plane_subspace(share, start, scale, count):
    rank, width = start.shape
    depth = rank * width // LANES // count
    slots = pltpu.VMEM((ITX, count, depth, LANES), jnp.float32)
    return pl.pallas_call(
        functools.partial(plane_kernel, count, scale),
        out_shape=jax.ShapeDtypeStruct(start.shape, jnp.float32),
        in_specs=in_vmem(2),
        out_specs=pl.BlockSpec(memory_space=pltpu.VMEM),
        scratch_shapes=[slots] * 3 + [pltpu.SemaphoreType.DMA((ITX, count))] * 4,
        compiler_params=pltpu.CompilerParams(
            collective_id=1, has_side_effects=True, vmem_limit_bytes=32 << 20
        ),
    )(share, start)


def exchange_kernel(count, snapshots, wide, pencils, parts, send, recv):
    greet(count)
    me = position()
    variables, planes, cells, window = snapshots.shape
    own = cells // count
    half = own // 2
    blocks = variables * planes

    def truncated(owner):
        here = pl.ds(pl.multiple_of(owner * own, own), own)
        rows = snapshots[:, :, here, :].reshape(blocks * own, window)
        pair = jnp.dot(rows, wide[...], preferred_element_type=jnp.float32)
        pair = pair.reshape(blocks, own, pair.shape[1])
        lanes = pair.shape[2] // 2
        packed = pair[:, :half, :lanes] + pair[:, half:, lanes:]
        return packed.reshape(blocks * half, lanes).astype(jnp.bfloat16)

    side = count // 2

    def partner(step):
        far = lax.rem(me // side + 1 - step // side, 2)
        return far * side + lax.rem(me + step, side)

    def copy(step):
        there = partner(step)
        return pltpu.make_async_remote_copy(
            src_ref=parts.at[there], dst_ref=pencils.at[me],
            send_sem=send.at[step], recv_sem=recv.at[step],
            device_id=place(there), device_id_type=MESH,
        )

    def begin(step, carry):
        there = partner(step)
        parts[there] = truncated(there)
        copy(step).start()
        return carry

    def finish(step, carry):
        copy(step).wait()
        return carry

    lax.fori_loop(0, side, begin, 0)
    lax.fori_loop(side + 1, count, begin, 0)
    pencils[me] = truncated(me)
    lax.fori_loop(0, side, finish, 0)
    lax.fori_loop(side + 1, count, finish, 0)


def exchange(snapshots, narrow, count):
    variables, planes, cells, window = snapshots.shape
    zero = jnp.zeros_like(narrow)
    wide = jnp.concatenate([narrow, zero, zero, narrow], axis=1)
    half = cells // count // 2
    shape = (count, variables * planes * half, 2 * narrow.shape[1])
    pencils = pl.pallas_call(
        functools.partial(exchange_kernel, count),
        out_shape=jax.ShapeDtypeStruct(shape, jnp.bfloat16),
        in_specs=in_vmem(2),
        out_specs=pl.BlockSpec(memory_space=pltpu.VMEM),
        scratch_shapes=[pltpu.VMEM(shape, jnp.bfloat16)]
        + [pltpu.SemaphoreType.DMA((count,))] * 2,
        compiler_params=pltpu.CompilerParams(
            collective_id=2, has_side_effects=True, vmem_limit_bytes=40 << 20
        ),
    )(snapshots, wide)
    pencils = pencils.reshape(count, variables, planes, half, shape[2])
    return pencils.transpose(1, 0, 2, 3, 4).reshape(variables, count * planes, half, shape[2])


def on_device(snapshots, start_time, start_plane):
    variables, planes, cell_count, window = snapshots.shape
    devices_all = lax.axis_size("blk") * lax.axis_size("pen")
    row_matrix = snapshots.reshape(variables * planes * cell_count, window)
    partial_time = jnp.dot(row_matrix.T, row_matrix, preferred_element_type=jnp.float32)
    time_rows = time_subspace(
        partial_time,
        start_time.T,
        1.0 / float(variables * planes * cell_count * devices_all),
        devices_all,
    )
    time_basis = time_rows.T
    time_narrow = time_basis.astype(jnp.bfloat16)
    pencils = exchange(snapshots, time_narrow, devices_all)
    column_total = float(variables * pencils.shape[2] * pencils.shape[3] * devices_all)
    partial_plane = jnp.einsum(
        "vxpl,vypl->xy", pencils, pencils, preferred_element_type=jnp.float32
    )
    plane_rows = plane_subspace(partial_plane, start_plane.T, 1.0 / column_total, devices_all)
    plane_basis = plane_rows.T
    plane_narrow = plane_basis.astype(jnp.bfloat16)
    core_blocks = jnp.einsum(
        "xk,vxpl->vkpl", plane_narrow, pencils, preferred_element_type=jnp.float32
    ).astype(jnp.bfloat16)
    rank = plane_narrow.shape[1]
    core_blocks = core_blocks.reshape(variables, rank, pencils.shape[2], 2, -1)
    core_tensor = core_blocks.transpose(0, 1, 3, 2, 4).reshape(variables, rank, -1)
    return (time_basis, plane_basis, core_tensor)


def solution(mesh):
    return jax.shard_map(
        on_device,
        mesh=mesh,
        in_specs=(P(None, ("blk", "pen"), None, None), P(), P()),
        out_specs=(P(), P(), P(None, None, ("blk", "pen"))),
        check_vma=False,
    )
```

```python
import functools

import jax
import jax.numpy as jnp
from jax import lax
from jax.experimental import pallas as pl
from jax.experimental.pallas import tpu as pltpu
from jax.sharding import PartitionSpec as P

ITT = 3
ITX = 3
LANES = 128
BLOCK = 8

HIGHEST = lax.Precision.HIGHEST
MESH = pl.DeviceIdType.MESH


def product(left, right, contract):
    return lax.dot_general(
        left, right, ((contract[:1], contract[1:]), ((), ())),
        precision=HIGHEST, preferred_element_type=jnp.float32,
    )


def inverse_factor(square):
    size = square.shape[0]
    rows = lax.broadcasted_iota(jnp.int32, (size, size), 0)
    columns = lax.broadcasted_iota(jnp.int32, (size, size), 1)
    wide = jnp.concatenate([square, (rows == columns).astype(jnp.float32)], axis=1)
    shape = (BLOCK, 2 * size)
    sublane = lax.broadcasted_iota(jnp.int32, shape, 0)
    panels = [wide[first : first + BLOCK] for first in range(0, size, BLOCK)]
    done = []
    for number, panel in enumerate(panels):
        first = number * BLOCK
        spread = {
            (later, j): jnp.broadcast_to(panels[later][:, first + j : first + j + 1], shape)
            for later in range(number, len(panels))
            for j in range(BLOCK)
        }
        row = [jnp.broadcast_to(panel[j : j + 1], shape) for j in range(BLOCK)]
        entry = {
            (i, j): jnp.broadcast_to(spread[number, j][i : i + 1], shape)
            for i in range(BLOCK)
            for j in range(i + 1)
        }
        scale, inverse = [], {}
        for j in range(BLOCK):
            scale.append(lax.rsqrt(entry[j, j]))
            for i in range(j + 1, BLOCK):
                entry[i, j] = entry[i, j] * scale[j]
            for i in range(j + 1, BLOCK):
                for t in range(j + 1, i + 1):
                    entry[i, t] = entry[i, t] - entry[i, j] * entry[t, j]
        for j in range(BLOCK):
            inverse[j, j] = scale[j]
            for i in range(j + 1, BLOCK):
                total = entry[i, j] * inverse[j, j]
                for t in range(j + 1, i):
                    total = total + entry[i, t] * inverse[t, j]
                inverse[i, j] = -scale[i] * total
        solved = [
            sum(inverse[i, t] * row[t] for t in range(i + 1)) for i in range(BLOCK)
        ]
        if number + 1 < len(panels):
            twice = [
                sum(inverse[i, t] * solved[i] for i in range(t, BLOCK)) for t in range(BLOCK)
            ]
            for later in range(number + 1, len(panels)):
                panels[later] = panels[later] - sum(
                    spread[later, t] * twice[t] for t in range(BLOCK)
                )
        joined = solved[0]
        for i in range(1, BLOCK):
            joined = jnp.where(sublane == i, solved[i], joined)
        done.append(joined)
    return jnp.concatenate(done, axis=0)[:, size:]


def cholesky_round(rows):
    return product(inverse_factor(product(rows, rows, (1, 1))), rows, (1, 0))


def place(index):
    pens = lax.axis_size("pen")
    return (index // pens, lax.rem(index, pens))


def position():
    return lax.axis_index("blk") * lax.axis_size("pen") + lax.axis_index("pen")


def greet(count):
    me = position()
    barrier = pltpu.get_barrier_semaphore()

    def signal(step, carry):
        pl.semaphore_signal(
            barrier, inc=1, device_id=place(lax.rem(me + step, count)), device_id_type=MESH
        )
        return carry

    lax.fori_loop(1, count, signal, 0)
    pl.semaphore_wait(barrier, count - 1)


def sum_over_devices(count, parts, landed, gathered, sems):
    me = position()
    send_a, recv_a, send_b, recv_b = sems

    def scatter(step):
        there = lax.rem(me + step, count)
        return pltpu.make_async_remote_copy(
            src_ref=parts.at[there], dst_ref=landed.at[step],
            send_sem=send_a.at[step], recv_sem=recv_a.at[step],
            device_id=place(there), device_id_type=MESH,
        )

    def spread(step):
        there = lax.rem(me + step, count)
        return pltpu.make_async_remote_copy(
            src_ref=gathered.at[me], dst_ref=gathered.at[me],
            send_sem=send_b.at[step], recv_sem=recv_b.at[step],
            device_id=place(there), device_id_type=MESH,
        )

    def each(action):
        def body(step, carry):
            action(step)
            return carry

        lax.fori_loop(1, count, body, 0)

    each(lambda step: scatter(step).start())
    each(lambda step: scatter(step).wait())
    total = parts[me]
    for step in range(1, count):
        total = total + landed[step]
    gathered[me] = total
    each(lambda step: spread(step).start())
    each(lambda step: spread(step).wait())


def time_kernel(count, scale, share, start, basis, parts, landed, gathered, gram, *sems):
    depth = parts.shape[1]
    for piece in range(count):
        parts[piece] = share[piece * depth : (piece + 1) * depth, :]
    greet(count)
    sum_over_devices(count, parts, landed, gathered, sems)
    for piece in range(count):
        gram[piece * depth : (piece + 1) * depth, :] = gathered[piece] * scale
    basis[...] = start[...]

    def sweep(step, carry):
        basis[...] = cholesky_round(product(basis[...], gram[...], (1, 0)))
        return carry

    lax.fori_loop(0, ITT, sweep, 0)
    basis[...] = cholesky_round(basis[...])


def plane_kernel(count, scale, gram, start, basis, parts, landed, gathered, *sems):
    greet(count)
    rank, width = start.shape
    depth = parts.shape[2]
    basis[...] = start[...]

    def sweep(step, carry):
        share = product(basis[...], gram[...], (1, 0)) * scale
        stack = jnp.concatenate(
            [share[:, first : first + LANES] for first in range(0, width, LANES)], axis=0
        )
        for piece in range(count):
            parts[step, piece] = stack[piece * depth : (piece + 1) * depth]
        sum_over_devices(
            count, parts.at[step], landed.at[step], gathered.at[step],
            [sem.at[step] for sem in sems],
        )
        flat = jnp.concatenate([gathered[step, piece] for piece in range(count)], axis=0)
        total = jnp.concatenate(
            [flat[first : first + rank] for first in range(0, flat.shape[0], rank)], axis=1
        )
        basis[...] = cholesky_round(total)
        return carry

    lax.fori_loop(0, ITX, sweep, 0)
    basis[...] = cholesky_round(basis[...])


def in_vmem(number):
    return [pl.BlockSpec(memory_space=pltpu.VMEM)] * number


def time_subspace(share, start, scale, count):
    window = share.shape[0]
    depth = window // count
    slots = pltpu.VMEM((count, depth, window), jnp.float32)
    return pl.pallas_call(
        functools.partial(time_kernel, count, scale),
        out_shape=jax.ShapeDtypeStruct(start.shape, jnp.float32),
        in_specs=in_vmem(2),
        out_specs=pl.BlockSpec(memory_space=pltpu.VMEM),
        scratch_shapes=[slots, slots, slots, pltpu.VMEM((window, window), jnp.float32)]
        + [pltpu.SemaphoreType.DMA((count,))] * 4,
        compiler_params=pltpu.CompilerParams(
            collective_id=0, has_side_effects=True, vmem_limit_bytes=32 << 20
        ),
    )(share, start)


def plane_subspace(share, start, scale, count):
    rank, width = start.shape
    depth = rank * width // LANES // count
    slots = pltpu.VMEM((ITX, count, depth, LANES), jnp.float32)
    return pl.pallas_call(
        functools.partial(plane_kernel, count, scale),
        out_shape=jax.ShapeDtypeStruct(start.shape, jnp.float32),
        in_specs=in_vmem(2),
        out_specs=pl.BlockSpec(memory_space=pltpu.VMEM),
        scratch_shapes=[slots] * 3 + [pltpu.SemaphoreType.DMA((ITX, count))] * 4,
        compiler_params=pltpu.CompilerParams(
            collective_id=1, has_side_effects=True, vmem_limit_bytes=32 << 20
        ),
    )(share, start)


def exchange_kernel(count, snapshots, wide, pencils, parts, send, recv):
    greet(count)
    me = position()
    variables, planes, cells, window = snapshots.shape
    own = cells // count
    half = own // 2
    blocks = variables * planes

    def truncated(owner):
        here = pl.ds(pl.multiple_of(owner * own, own), own)
        rows = snapshots[:, :, here, :].reshape(blocks * own, window)
        pair = jnp.dot(rows, wide[...], preferred_element_type=jnp.float32)
        pair = pair.reshape(blocks, own, pair.shape[1])
        lanes = pair.shape[2] // 2
        packed = pair[:, :half, :lanes] + pair[:, half:, lanes:]
        return packed.reshape(blocks * half, lanes).astype(jnp.bfloat16)

    side = count // 2

    def partner(step):
        far = lax.rem(me // side + 1 - step // side, 2)
        return far * side + lax.rem(me + step, side)

    def copy(step):
        there = partner(step)
        return pltpu.make_async_remote_copy(
            src_ref=parts.at[there], dst_ref=pencils.at[me],
            send_sem=send.at[step], recv_sem=recv.at[step],
            device_id=place(there), device_id_type=MESH,
        )

    def begin(step, carry):
        there = partner(step)
        parts[there] = truncated(there)
        copy(step).start()
        return carry

    def finish(step, carry):
        copy(step).wait()
        return carry

    def begin_two(step, carry):
        return begin(side + 1 + step, begin(step, carry))

    lax.fori_loop(0, side - 1, begin_two, 0)
    begin(side - 1, 0)
    pencils[me] = truncated(me)
    lax.fori_loop(0, side, finish, 0)
    lax.fori_loop(side + 1, count, finish, 0)


def exchange(snapshots, narrow, count):
    variables, planes, cells, window = snapshots.shape
    zero = jnp.zeros_like(narrow)
    wide = jnp.concatenate([narrow, zero, zero, narrow], axis=1)
    half = cells // count // 2
    shape = (count, variables * planes * half, 2 * narrow.shape[1])
    pencils = pl.pallas_call(
        functools.partial(exchange_kernel, count),
        out_shape=jax.ShapeDtypeStruct(shape, jnp.bfloat16),
        in_specs=in_vmem(2),
        out_specs=pl.BlockSpec(memory_space=pltpu.VMEM),
        scratch_shapes=[pltpu.VMEM(shape, jnp.bfloat16)]
        + [pltpu.SemaphoreType.DMA((count,))] * 2,
        compiler_params=pltpu.CompilerParams(
            collective_id=2, has_side_effects=True, vmem_limit_bytes=40 << 20
        ),
    )(snapshots, wide)
    pencils = pencils.reshape(count, variables, planes, half, shape[2])
    return pencils.transpose(1, 0, 2, 3, 4).reshape(variables, count * planes, half, shape[2])


def on_device(snapshots, start_time, start_plane):
    variables, planes, cell_count, window = snapshots.shape
    devices_all = lax.axis_size("blk") * lax.axis_size("pen")
    row_matrix = snapshots.reshape(variables * planes * cell_count, window)
    partial_time = jnp.dot(row_matrix.T, row_matrix, preferred_element_type=jnp.float32)
    time_rows = time_subspace(
        partial_time,
        start_time.T,
        1.0 / float(variables * planes * cell_count * devices_all),
        devices_all,
    )
    time_basis = time_rows.T
    time_narrow = time_basis.astype(jnp.bfloat16)
    pencils = exchange(snapshots, time_narrow, devices_all)
    column_total = float(variables * pencils.shape[2] * pencils.shape[3] * devices_all)
    partial_plane = jnp.einsum(
        "vxpl,vypl->xy", pencils, pencils, preferred_element_type=jnp.float32
    )
    plane_rows = plane_subspace(partial_plane, start_plane.T, 1.0 / column_total, devices_all)
    plane_basis = plane_rows.T
    plane_narrow = plane_basis.astype(jnp.bfloat16)
    core_blocks = jnp.einsum(
        "xk,vxpl->vkpl", plane_narrow, pencils, preferred_element_type=jnp.float32
    ).astype(jnp.bfloat16)
    rank = plane_narrow.shape[1]
    core_blocks = core_blocks.reshape(variables, rank, pencils.shape[2], 2, -1)
    core_tensor = core_blocks.transpose(0, 1, 3, 2, 4).reshape(variables, rank, -1)
    return (time_basis, plane_basis, core_tensor)


def solution(mesh):
    return jax.shard_map(
        on_device,
        mesh=mesh,
        in_specs=(P(None, ("blk", "pen"), None, None), P(), P()),
        out_specs=(P(), P(), P(None, None, ("blk", "pen"))),
        check_vma=False,
    )
```
